32 devices in a mesh: gx: 16 (over z, y, x), gy: 2 (over core).
Axes of the slice: x: 2, y: 2, z: 4, core: 2. Of those that a mesh axis runs over, the one named last changes fastest.
Arguments:
- checkpoints: bfloat16 [4, 27, 64, 16, 128], P(None, None, 'gx', 'gy'), may hold values from 0 to 1, as said below
- step_ckpt: int32 [3], replicated, may hold values from 0 to 3, as said below
- solid_mask: int32 [64, 16, 128], P('gx', 'gy'), may hold values from 0 to 1, as said below
- omega: float32 [64, 16, 128], P('gx', 'gy'), may hold values from 0.7 to 1.9
- adjoint_init: float32 [27, 64, 16, 128], P(None, 'gx', 'gy'), may hold values from -150 to 150
Outputs:
- adjoint: float32 [27, 64, 16, 128], P(None, 'gx', 'gy')
- sensitivity: float32 [64, 16, 128], P('gx', 'gy')
- growth: float32 [3], replicated
The draws below stay inside these ranges and needn't reach their ends.
Inputs may be any that keep to these rules, and one draw needn't show every extreme that they name: `checkpoints`: positive populations, each checkpoint near equilibrium at low Mach number. `step_ckpt`: distinct checkpoint numbers; the first and the last checkpoint are always among them. `solid_mask`: the cells of one solid sphere are 1, all others 0.
All inputs are finite; a program needn't handle non-finite values.
Results may differ from the reference program's by a relative error of at most 0.00075.
Values sent between devices are 32-bit elements; how exact they have to be, the bound alone decides.
A program may use at most 64 MiB of HBM per device.

```python
import math
import jax
import jax.numpy as jnp
import numpy as np
from jax import lax

STEPS = 3
NCK = 4
NX = 64
NY = 16
NZ = 128


DIRECTIONS = np.array([[a, b, c] for a in (-1, 0, 1) for b in (-1, 0, 1) for c in (-1, 0, 1)], dtype=np.float32)


WEIGHTS = np.array([8.0 / 27.0, 2.0 / 27.0, 1.0 / 54.0, 1.0 / 216.0], dtype=np.float32)[np.sum(np.abs(DIRECTIONS), axis=1).astype(np.int32)]


def draw_checkpoints(key, part):
    key_rho, key_vel, key_noise = jax.random.split(key, 3)
    rho = 1.0 + 0.1 * jax.random.uniform(key_rho, (NCK, 1, NX, NY, NZ), jnp.float32, -1.0, 1.0)
    vel = jax.random.uniform(key_vel, (3, NCK, 1, NX, NY, NZ), jnp.float32, -0.08, 0.08)
    along = jnp.zeros((NCK, 27, NX, NY, NZ), jnp.float32)
    for axis_num in range(3):
        along = along + jnp.asarray(DIRECTIONS[:, axis_num]).reshape(1, 27, 1, 1, 1) * vel[axis_num]
    square = vel[0] * vel[0] + vel[1] * vel[1] + vel[2] * vel[2]
    feq = jnp.asarray(WEIGHTS).reshape(1, 27, 1, 1, 1) * rho * (1.0 + 3.0 * along + 4.5 * along * along - 1.5 * square)
    noise = 0.3 * jax.random.uniform(key_noise, feq.shape, jnp.float32, -1.0, 1.0)
    return (feq * (1.0 + noise)).astype(jnp.bfloat16)


def draw_step_ckpt(key, part):
    key_inner, key_order = jax.random.split(key)
    inner = 1 + jax.random.permutation(key_inner, NCK - 2)[:STEPS - 2].astype(jnp.int32)
    values = jnp.concatenate([jnp.array([0, NCK - 1], jnp.int32), inner])
    order = jax.random.permutation(key_order, STEPS)
    return values[order].astype(jnp.int32)


def draw_solid_mask(key, part):
    keys = jax.random.split(key, 4)
    center_x = jax.random.randint(keys[0], (), 0, NX)
    center_y = jax.random.randint(keys[1], (), 0, NY)
    center_z = jax.random.randint(keys[2], (), 0, NZ)
    radius = jax.random.randint(keys[3], (), max(2, NY // 8), max(3, NY // 4) + 1)
    dist_x = jnp.arange(NX, dtype=jnp.int32) - center_x
    dist_y = jnp.arange(NY, dtype=jnp.int32) - center_y
    dist_z = jnp.arange(NZ, dtype=jnp.int32) - center_z
    total = dist_x[:, None, None] ** 2 + dist_y[None, :, None] ** 2 + dist_z[None, None, :] ** 2
    return (total <= radius * radius).astype(jnp.int32)


def draw_adjoint_init(key, part):
    key_base, key_col = jax.random.split(key)
    pos_x = jnp.arange(NX, dtype=jnp.float32) / NX
    pos_y = jnp.arange(NY, dtype=jnp.float32) / NY
    scale = (0.5 + pos_x)[:, None, None] * (0.5 + pos_y)[None, :, None]
    col = jnp.exp(jax.random.uniform(key_col, (NX, NY, 1), jnp.float32) * jnp.log(10.0))
    base = jnp.clip(jax.random.normal(key_base, (27, NX, NY, NZ), jnp.float32), -4.0, 4.0)
    return base * scale * col


def block_scale(key, dims, cuts, low, largest):
    level, own = 1.0, jax.random.fold_in(key, 6)
    for position, shards_of in cuts:
        heights = jnp.exp(jax.random.uniform(jax.random.fold_in(own, position), (shards_of,), jnp.float32, low / len(cuts), largest / len(cuts)))
        level = level * jnp.repeat(heights, dims[position] // shards_of).reshape([-1 if axis == position else 1 for axis in range(len(dims))])
    return level


def setup_inputs(seed: int = 0) -> dict:
    seeds = jax.random.split(jax.random.key(seed), 6)
    return {
        "checkpoints": draw_checkpoints(jax.random.fold_in(seeds[5], 71), 0),
        "step_ckpt": draw_step_ckpt(jax.random.fold_in(seeds[5], 71), 0),
        "solid_mask": draw_solid_mask(jax.random.fold_in(seeds[5], 71), 0),
        "omega": jnp.clip(jnp.exp(math.log(1.9) - 0.99852883 * jax.random.uniform(seeds[3], (NX, NY, NZ), jnp.float32) ** block_scale(seeds[3], (NX, NY, NZ), ((0, 16), (1, 2)), -0.2, 0.2)), 0.7, 1.9),
        "adjoint_init": draw_adjoint_init(jax.random.fold_in(seeds[5], 71), 0),
    }


DIRECTIONS = np.array([[a, b, c] for a in (-1, 0, 1) for b in (-1, 0, 1) for c in (-1, 0, 1)], dtype=np.float32)
WEIGHTS = np.array([8.0 / 27.0, 2.0 / 27.0, 1.0 / 54.0, 1.0 / 216.0], dtype=np.float32)[np.sum(np.abs(DIRECTIONS), axis=1).astype(np.int32)]

def column(values):
    return jnp.asarray(values, jnp.float32).reshape(27, 1, 1, 1)

def equilibrium(base):
    rho = lax.optimization_barrier(jnp.sum(base, axis=0))
    speeds = []
    for axis_num in range(3):
        speeds.append(lax.optimization_barrier(jnp.sum(column(DIRECTIONS[:, axis_num]) * base, axis=0)) / rho)
    along = column(DIRECTIONS[:, 0]) * speeds[0] + column(DIRECTIONS[:, 1]) * speeds[1] + column(DIRECTIONS[:, 2]) * speeds[2]
    square = speeds[0] * speeds[0] + speeds[1] * speeds[1] + speeds[2] * speeds[2]
    return column(WEIGHTS) * rho * (1.0 + 3.0 * along + 4.5 * along * along - 1.5 * square)

def collide(base, omega, fluid):
    post = base - omega * (base - equilibrium(base))
    return jnp.where(fluid, post, base[::-1])

def stream(field):
    moved = []
    for index in range(27):
        shift_by = tuple((int(v) for v in DIRECTIONS[index]))
        moved.append(jnp.roll(field[index], shift_by, axis=(0, 1, 2)))
    return jnp.stack(moved)

def reference(checkpoints, step_ckpt, solid_mask, omega, adjoint_init):
    fluid = solid_mask == 0
    adjoint = adjoint_init
    sensitivity = jnp.zeros(omega.shape, jnp.float32)
    growth = []
    for step in range(STEPS):
        base = checkpoints[step_ckpt[step]].astype(jnp.float32)
        _, backward = jax.vjp(lambda f, rate: stream(collide(f, rate, fluid)), base, omega)
        previous, d_rate = backward(adjoint)
        sensitivity = sensitivity - 3.0 * omega * omega * d_rate
        factor = jnp.sqrt(jnp.mean(previous * previous) + 1e-06)
        adjoint = previous / factor
        growth.append(factor)
    return (adjoint, sensitivity, jnp.stack(growth))
```

```python
import functools

import jax
import jax.numpy as jnp
from jax import lax
from jax.experimental import pallas as pl
from jax.experimental.pallas import tpu as pltpu
from jax.sharding import PartitionSpec as P

MESH = pl.DeviceIdType.MESH
EDGE = 16
CORNERS = ((0, 0), (0, 1), (1, 0), (1, 1))


def three(minus, plain, plus):
    even = plus + minus
    return 4.0 * plain + even, plus - minus, even


def weighted_moments(p):
    along_z = [three(*p[3 * k : 3 * k + 3]) for k in range(9)]
    along_y = []
    for a in range(3):
        rows = along_z[3 * a : 3 * a + 3]
        y0 = three(*[r[0] for r in rows])
        y1 = three(*[r[1] for r in rows])
        y2 = three(*[r[2] for r in rows])
        along_y.append((y0[0], y0[1], y0[2], y1[0], y1[1], y2[0]))
    m, my, myy, mz, myz, mzz = (three(*[r[k] for r in along_y]) for k in range(6))
    return m[0], m[1], my[0], mz[0], m[2], myy[0], mzz[0], my[1], mz[1], myz[0]


def plain_moments(f):
    zs = [(f[3 * k] + f[3 * k + 2] + f[3 * k + 1], f[3 * k + 2] - f[3 * k]) for k in range(9)]
    ys = []
    for a in range(3):
        r = zs[3 * a : 3 * a + 3]
        ys.append((r[0][0] + r[2][0] + r[1][0], r[2][0] - r[0][0], r[0][1] + r[1][1] + r[2][1]))
    total = [ys[0][k] + ys[1][k] + ys[2][k] for k in range(3)]
    return total[0], ys[2][0] - ys[0][0], total[1], total[2]


def kernel(
    steps, nx, ny, nz, ngx, ngy,
    idx_ref, ck_hbm, solid_hbm, omega_hbm, adj_hbm,
    out_ref, sens_ref, growth_ref,
    ck_ref, solid_ref, omega_ref, adj_ref,
    fld, ysend, yrecv, fval, mom, terms, acc_ref, line_y, line_x, own_y, own_x,
    local_sem, send_sem, recv_sem, ysum_send, ysum_recv, xsum_send, xsum_recv,
):
    gx, gy = lax.axis_index("gx"), lax.axis_index("gy")
    plane = 27 * ny

    def gxs(k):
        return lax.rem(gx + (k + ngx), ngx)

    def gys(k):
        return lax.rem(gy + (k + ngy), ngy)

    loads = [
        pltpu.make_async_copy(src, dst, local_sem.at[n])
        for n, (src, dst) in enumerate(
            ((adj_hbm, adj_ref), (ck_hbm, ck_ref), (solid_hbm, solid_ref), (omega_hbm, omega_ref))
        )
    ]
    for copy in loads:
        copy.start()

    barrier = pltpu.get_barrier_semaphore()
    greeted = (
        [(gxs(k), gy) for k in range(1, ngx)]
        + [(gx, gys(k)) for k in range(1, ngy)]
        + [(gxs(a), gys(b)) for a in (-1, 1) for b in (-1, 1)]
    )
    for device in greeted:
        pl.semaphore_signal(barrier, inc=1, device_id=device, device_id_type=MESH)

    loads[0].wait()
    for x in range(nx):
        for i in range(27):
            fld[0, pl.ds((x + 1) * plane + i * ny, ny), :] = adj_ref[i, x]

    def pack(s):
        for x in range(nx):
            for d in (0, 1):
                row = 0 if d == 1 else ny - 1
                for a in range(3):
                    start = (x + 1) * plane + (9 * a + 6 * d) * ny + row
                    ysend[s, d, pl.ds(x * EDGE + 4 * a, 3), :] = fld[s, pl.ds(start, 3, stride=ny), :]

    def copies(s):
        todo = [
            (fld.at[s, pl.ds(nx * plane, 9 * ny), :], fld.at[s, pl.ds(0, 9 * ny), :], (gxs(1), gy)),
            (
                fld.at[s, pl.ds(plane + 18 * ny, 9 * ny), :],
                fld.at[s, pl.ds((nx + 1) * plane + 18 * ny, 9 * ny), :],
                (gxs(-1), gy),
            ),
        ]
        for d in (0, 1):
            todo.append(
                (ysend.at[s, d], yrecv.at[s, d, pl.ds(EDGE, nx * EDGE), :], (gx, gys(1 - 2 * d)))
            )
        for a, d in CORNERS:
            src = 8 if a else (nx - 1) * EDGE
            dst = (nx + 1) * EDGE + 8 if a else 0
            todo.append(
                (
                    ysend.at[s, d, pl.ds(src, 8), :],
                    yrecv.at[s, d, pl.ds(dst, 8), :],
                    (gxs(1 - 2 * a), gys(1 - 2 * d)),
                )
            )
        return [
            pltpu.make_async_remote_copy(
                src_ref=src,
                dst_ref=dst,
                send_sem=send_sem.at[s, n],
                recv_sem=recv_sem.at[s, n],
                device_id=device,
                device_id_type=MESH,
            )
            for n, (src, dst, device) in enumerate(todo)
        ]

    def base_moments(s):
        which = idx_ref[s]

        def pair(k, _):
            rows = pl.ds(pl.multiple_of(k * 2 * ny, 2 * ny), 2 * ny)
            f = [ck_ref[which, i, rows, :].astype(jnp.float32) for i in range(27)]
            for i in range(27):
                fval[s, i, rows, :] = f[i]
            rho, jx, jy, jz = plain_moments(f)
            inv = 1.0 / rho
            for n, value in enumerate((rho, jx * inv, jy * inv, jz * inv)):
                mom[s, n, rows, :] = value
            return 0

        lax.fori_loop(0, nx // 2, pair, 0)

    lane_row = lax.broadcasted_iota(jnp.int32, (ny, nz), 0)
    first, last = lane_row == 0, lane_row == ny - 1

    def step_plane(s, x):
        p = []
        for i in range(27):
            a, b, c = i // 9, i // 3 % 3, i % 3
            start = pl.multiple_of((x + a) * plane + i * ny, ny)
            tile = fld[s, pl.ds(start, ny), :]
            if b != 1:
                edge = yrecv[s, b // 2, pl.ds((x + a) * EDGE + 4 * a + c, 1), :]
                tile = jnp.where(first if b == 2 else last, jnp.broadcast_to(edge, (ny, nz)), tile)
                tile = pltpu.roll(tile, ny - 1 if b == 2 else 1, 0)
            if c != 1:
                tile = pltpu.roll(tile, nz - 1 if c == 2 else 1, 1)
            p.append(tile)
        rows = pl.ds(pl.multiple_of(x * ny, ny), ny)
        rho, ux, uy, uz = (mom[s, n, rows, :] for n in range(4))
        omega = omega_ref[rows, :]
        fluid = solid_ref[rows, :] == 0
        m0, mx, my, mz, mxx, myy, mzz, mxy, mxz, myz = weighted_moments(p)
        vx = mxx * ux + mxy * uy + mxz * uz
        vy = mxy * ux + myy * uy + myz * uz
        vz = mxz * ux + myz * uy + mzz * uz
        square = ux * ux + uy * uy + uz * uz
        um = ux * mx + uy * my + uz * mz
        uv = ux * vx + uy * vy + uz * vz
        scale = 1.0 / 216.0
        total = scale * (m0 * (1.0 - 1.5 * square) + 3.0 * um + 4.5 * uv)
        gxv = scale * (3.0 * (mx - ux * m0) + 9.0 * vx)
        gyv = scale * (3.0 * (my - uy * m0) + 9.0 * vy)
        gzv = scale * (3.0 * (mz - uz * m0) + 9.0 * vz)
        base = omega * (total - (ux * gxv + uy * gyv + uz * gzv))
        wx, wy, wz = omega * gxv, omega * gyv, omega * gzv
        keep = 1.0 - omega
        square_sum = None
        for a in range(3):
            ta = base if a == 1 else (base + wx if a == 2 else base - wx)
            for b in range(3):
                tb = ta if b == 1 else (ta + wy if b == 2 else ta - wy)
                for c in range(3):
                    tc = tb if c == 1 else (tb + wz if c == 2 else tb - wz)
                    i = 9 * a + 3 * b + c
                    value = jnp.where(fluid, keep * p[i] + tc, p[26 - i])
                    start = pl.multiple_of((x + 1) * plane + i * ny, ny)
                    fld[s + 1, pl.ds(start, ny), :] = value
                    square_sum = value * value if square_sum is None else square_sum + value * value
        pf = None
        for i in range(27):
            product = p[i] * fval[s, i, rows, :]
            pf = product if pf is None else pf + product
        terms[s, rows, :] = jnp.where(fluid, 3.0 * omega * omega * (pf - rho * total), 0.0)
        acc_ref[s] += square_sum

    acc_ref[...] = jnp.zeros_like(acc_ref)
    pack(0)
    pl.semaphore_wait(barrier, len(greeted))

    sent = []
    for s in range(steps):
        moving = copies(s)
        sent += moving
        for copy in moving:
            copy.start()
        if s == 0:
            for copy in loads[1:]:
                copy.wait()
        base_moments(s)
        for copy in moving[2:4]:
            copy.wait_recv()
        lax.fori_loop(1, nx - 1, lambda x, _, s=s: (step_plane(s, x), 0)[1], 0)
        for copy in moving[:2] + moving[4:]:
            copy.wait_recv()
        lax.fori_loop(0, 2, lambda t, _, s=s: (step_plane(s, t * (nx - 1)), 0)[1], 0)
        if s + 1 < steps:
            pack(s + 1)

    lane = lax.broadcasted_iota(jnp.int32, (1, nz), 1)
    row = jnp.zeros((1, nz), jnp.float32)
    for s in range(steps):
        value = jnp.sum(jnp.sum(acc_ref[s], axis=0, keepdims=True), axis=1, keepdims=True)
        row = row + jnp.where(lane == s, value, 0.0)

    def spread(row, own, line, me, count, send, recv, place):
        own[0] = row
        copies = [
            pltpu.make_async_remote_copy(
                src_ref=own.at[0],
                dst_ref=line.at[k - 1],
                send_sem=send.at[k - 1],
                recv_sem=recv.at[k - 1],
                device_id=place(k),
                device_id_type=MESH,
            )
            for k in range(1, count)
        ]
        for copy in copies:
            copy.start()
        for copy in copies:
            copy.wait_recv()
        for k in range(count - 1):
            row = row + line[k]
        return row, copies

    row, more = spread(row, own_y, line_y, gy, ngy, ysum_send, ysum_recv, lambda k: (gx, gys(k)))
    sent += more
    row, more = spread(row, own_x, line_x, gx, ngx, xsum_send, xsum_recv, lambda k: (gxs(k), gy))
    sent += more

    inverse = jnp.ones((1, nz), jnp.float32)
    sens = jnp.zeros((nx * ny, nz), jnp.float32)
    count = float(27 * nx * ny * nz * ngx * ngy)
    for s in range(steps):
        sens = sens + terms[s] * inverse
        total = jnp.sum(jnp.where(lane == s, row, 0.0), axis=1, keepdims=True)
        total = jnp.broadcast_to(total, (1, nz))
        factor = jnp.sqrt(total * (inverse * inverse) * (1.0 / count) + 1e-06)
        inverse = inverse / factor
        growth_ref[pl.ds(s, 1), :] = factor
    sens_ref[...] = sens
    for x in range(nx):
        for i in range(27):
            out_ref[i, x] = fld[steps, pl.ds((x + 1) * plane + i * ny, ny), :] * inverse
    for copy in sent:
        copy.wait_send()


def body(checkpoints, step_ckpt, solid_mask, omega, adjoint_init):
    nck, _, nx, ny, nz = checkpoints.shape
    steps = step_ckpt.shape[0]
    ngx, ngy = lax.axis_size("gx"), lax.axis_size("gy")
    f32 = jnp.float32
    hbm = pl.BlockSpec(memory_space=pltpu.HBM)
    vmem = pl.BlockSpec(memory_space=pltpu.VMEM)
    dma = pltpu.SemaphoreType.DMA
    rows = (nx + 2) * 27 * ny
    out, sens, growth = pl.pallas_call(
        functools.partial(kernel, steps, nx, ny, nz, ngx, ngy),
        out_shape=(
            jax.ShapeDtypeStruct(adjoint_init.shape, f32),
            jax.ShapeDtypeStruct((nx * ny, nz), f32),
            jax.ShapeDtypeStruct((steps, nz), f32),
        ),
        in_specs=[pl.BlockSpec(memory_space=pltpu.SMEM), hbm, hbm, hbm, hbm],
        out_specs=(vmem, vmem, vmem),
        scratch_shapes=[
            pltpu.VMEM((nck, 27, nx * ny, nz), checkpoints.dtype),
            pltpu.VMEM((nx * ny, nz), jnp.int32),
            pltpu.VMEM((nx * ny, nz), f32),
            pltpu.VMEM(adjoint_init.shape, f32),
            pltpu.VMEM((steps + 1, rows, nz), f32),
            pltpu.VMEM((steps, 2, nx * EDGE, nz), f32),
            pltpu.VMEM((steps, 2, (nx + 2) * EDGE, nz), f32),
            pltpu.VMEM((steps, 27, nx * ny, nz), f32),
            pltpu.VMEM((steps, 4, nx * ny, nz), f32),
            pltpu.VMEM((steps, nx * ny, nz), f32),
            pltpu.VMEM((steps, ny, nz), f32),
            pltpu.VMEM((max(ngy - 1, 1), 1, nz), f32),
            pltpu.VMEM((max(ngx - 1, 1), 1, nz), f32),
            pltpu.VMEM((1, 1, nz), f32),
            pltpu.VMEM((1, 1, nz), f32),
            dma((4,)),
            dma((steps, 8)),
            dma((steps, 8)),
            dma((max(ngy - 1, 1),)),
            dma((max(ngy - 1, 1),)),
            dma((max(ngx - 1, 1),)),
            dma((max(ngx - 1, 1),)),
        ],
        compiler_params=pltpu.CompilerParams(
            collective_id=0, has_side_effects=True, vmem_limit_bytes=60 * 1024 * 1024
        ),
        cost_estimate=pl.CostEstimate(flops=10**7, bytes_accessed=2 * 10**6, transcendentals=0),
    )(
        step_ckpt,
        checkpoints.reshape(nck, 27, nx * ny, nz),
        solid_mask.reshape(nx * ny, nz),
        omega.reshape(nx * ny, nz),
        adjoint_init,
    )
    return out, sens.reshape(omega.shape), growth[:, 0]


def solution(mesh):
    in_specs = (
        P(None, None, "gx", "gy", None),
        P(),
        P("gx", "gy", None),
        P("gx", "gy", None),
        P(None, "gx", "gy", None),
    )
    out_specs = (P(None, "gx", "gy", None), P("gx", "gy", None), P())
    return jax.shard_map(body, mesh=mesh, in_specs=in_specs, out_specs=out_specs, check_vma=False)
```

```python
import functools

import jax
import jax.numpy as jnp
from jax import lax
from jax.experimental import pallas as pl
from jax.experimental.pallas import tpu as pltpu
from jax.sharding import PartitionSpec as P

MESH = pl.DeviceIdType.MESH
EDGE = 16
CORNERS = ((0, 0), (0, 1), (1, 0), (1, 1))


def three(minus, plain, plus):
    even = plus + minus
    return 4.0 * plain + even, plus - minus, even


def weighted_moments(p):
    along_z = [three(*p[3 * k : 3 * k + 3]) for k in range(9)]
    along_y = []
    for a in range(3):
        rows = along_z[3 * a : 3 * a + 3]
        y0 = three(*[r[0] for r in rows])
        y1 = three(*[r[1] for r in rows])
        y2 = three(*[r[2] for r in rows])
        along_y.append((y0[0], y0[1], y0[2], y1[0], y1[1], y2[0]))
    m, my, myy, mz, myz, mzz = (three(*[r[k] for r in along_y]) for k in range(6))
    return m[0], m[1], my[0], mz[0], m[2], myy[0], mzz[0], my[1], mz[1], myz[0]


def plain_moments(f):
    zs = [(f[3 * k] + f[3 * k + 2] + f[3 * k + 1], f[3 * k + 2] - f[3 * k]) for k in range(9)]
    ys = []
    for a in range(3):
        r = zs[3 * a : 3 * a + 3]
        ys.append((r[0][0] + r[2][0] + r[1][0], r[2][0] - r[0][0], r[0][1] + r[1][1] + r[2][1]))
    total = [ys[0][k] + ys[1][k] + ys[2][k] for k in range(3)]
    return total[0], ys[2][0] - ys[0][0], total[1], total[2]


def kernel(
    steps, nx, ny, nz, ngx, ngy,
    idx_hbm, ck_hbm, solid_hbm, omega_hbm, adj_hbm,
    raw_hbm, terms_hbm, sums_hbm,
    idx_ref, ck_ref, solid_ref, omega_ref, adj_ref,
    fld, ysend, yrecv, fval, mom, terms, acc_ref, line, own,
    local_sem, send_sem, recv_sem, sum_send, sum_recv,
):
    gx, gy = lax.axis_index("gx"), lax.axis_index("gy")
    plane = 27 * ny

    def gxs(k):
        return lax.rem(gx + (k + ngx), ngx)

    def gys(k):
        return lax.rem(gy + (k + ngy), ngy)

    loads = [
        pltpu.make_async_copy(src, dst, local_sem.at[n])
        for n, (src, dst) in enumerate(
            (
                (adj_hbm, adj_ref),
                (ck_hbm, ck_ref),
                (solid_hbm, solid_ref),
                (omega_hbm, omega_ref),
                (idx_hbm, idx_ref),
            )
        )
    ]
    barrier = pltpu.get_barrier_semaphore()
    here = gx * ngy + gy
    every = ngx * ngy
    others = []
    for k in range(1, every):
        there = lax.rem(here + k, every)
        others.append((there // ngy, lax.rem(there, ngy)))
    greeted = others
    for device in greeted:
        pl.semaphore_signal(barrier, inc=1, device_id=device, device_id_type=MESH)

    for copy in loads:
        copy.start()
    loads[0].wait()
    for x in range(nx):
        for i in range(27):
            fld[0, pl.ds((x + 1) * plane + i * ny, ny), :] = adj_ref[i, x]

    def pack(s):
        for x in range(nx):
            for d in (0, 1):
                row = 0 if d == 1 else ny - 1
                for a in range(3):
                    start = (x + 1) * plane + (9 * a + 6 * d) * ny + row
                    ysend[s, d, pl.ds(x * EDGE + 4 * a, 3), :] = fld[s, pl.ds(start, 3, stride=ny), :]

    def copies(s):
        todo = [
            (fld.at[s, pl.ds(nx * plane, 9 * ny), :], fld.at[s, pl.ds(0, 9 * ny), :], (gxs(1), gy)),
            (
                fld.at[s, pl.ds(plane + 18 * ny, 9 * ny), :],
                fld.at[s, pl.ds((nx + 1) * plane + 18 * ny, 9 * ny), :],
                (gxs(-1), gy),
            ),
        ]
        for d in (0, 1):
            todo.append(
                (ysend.at[s, d], yrecv.at[s, d, pl.ds(EDGE, nx * EDGE), :], (gx, gys(1 - 2 * d)))
            )
        for a, d in CORNERS:
            src = 8 if a else (nx - 1) * EDGE
            dst = (nx + 1) * EDGE + 8 if a else 0
            todo.append(
                (
                    ysend.at[s, d, pl.ds(src, 8), :],
                    yrecv.at[s, d, pl.ds(dst, 8), :],
                    (gxs(1 - 2 * a), gys(1 - 2 * d)),
                )
            )
        return [
            pltpu.make_async_remote_copy(
                src_ref=src,
                dst_ref=dst,
                send_sem=send_sem.at[s, n],
                recv_sem=recv_sem.at[s, n],
                device_id=device,
                device_id_type=MESH,
            )
            for n, (src, dst, device) in enumerate(todo)
        ]

    def base_moments(s):
        which = idx_ref[s]

        def pair(k, _):
            rows = pl.ds(pl.multiple_of(k * 2 * ny, 2 * ny), 2 * ny)
            f = [ck_ref[which, i, rows, :].astype(jnp.float32) for i in range(27)]
            for i in range(27):
                fval[s, i, rows, :] = f[i]
            rho, jx, jy, jz = plain_moments(f)
            inv = 1.0 / rho
            for n, value in enumerate((rho, jx * inv, jy * inv, jz * inv)):
                mom[s, n, rows, :] = value
            return 0

        lax.fori_loop(0, nx // 2, pair, 0)

    lane_row = lax.broadcasted_iota(jnp.int32, (ny, nz), 0)
    first, last = lane_row == 0, lane_row == ny - 1

    def step_plane(s, x):
        p = []
        for i in range(27):
            a, b, c = i // 9, i // 3 % 3, i % 3
            start = pl.multiple_of((x + a) * plane + i * ny, ny)
            tile = fld[s, pl.ds(start, ny), :]
            if b != 1:
                edge = yrecv[s, b // 2, pl.ds((x + a) * EDGE + 4 * a + c, 1), :]
                tile = jnp.where(first if b == 2 else last, jnp.broadcast_to(edge, (ny, nz)), tile)
                tile = pltpu.roll(tile, ny - 1 if b == 2 else 1, 0)
            if c != 1:
                tile = pltpu.roll(tile, nz - 1 if c == 2 else 1, 1)
            p.append(tile)
        rows = pl.ds(pl.multiple_of(x * ny, ny), ny)
        rho, ux, uy, uz = (mom[s, n, rows, :] for n in range(4))
        omega = omega_ref[rows, :]
        fluid = solid_ref[rows, :] == 0
        m0, mx, my, mz, mxx, myy, mzz, mxy, mxz, myz = weighted_moments(p)
        vx = mxx * ux + mxy * uy + mxz * uz
        vy = mxy * ux + myy * uy + myz * uz
        vz = mxz * ux + myz * uy + mzz * uz
        square = ux * ux + uy * uy + uz * uz
        um = ux * mx + uy * my + uz * mz
        uv = ux * vx + uy * vy + uz * vz
        scale = 1.0 / 216.0
        total = scale * (m0 * (1.0 - 1.5 * square) + 3.0 * um + 4.5 * uv)
        gxv = scale * (3.0 * (mx - ux * m0) + 9.0 * vx)
        gyv = scale * (3.0 * (my - uy * m0) + 9.0 * vy)
        gzv = scale * (3.0 * (mz - uz * m0) + 9.0 * vz)
        base = omega * (total - (ux * gxv + uy * gyv + uz * gzv))
        wx, wy, wz = omega * gxv, omega * gyv, omega * gzv
        keep = 1.0 - omega
        square_sum = None
        for a in range(3):
            ta = base if a == 1 else (base + wx if a == 2 else base - wx)
            for b in range(3):
                tb = ta if b == 1 else (ta + wy if b == 2 else ta - wy)
                for c in range(3):
                    tc = tb if c == 1 else (tb + wz if c == 2 else tb - wz)
                    i = 9 * a + 3 * b + c
                    value = jnp.where(fluid, keep * p[i] + tc, p[26 - i])
                    start = pl.multiple_of((x + 1) * plane + i * ny, ny)
                    fld[s + 1, pl.ds(start, ny), :] = value
                    square_sum = value * value if square_sum is None else square_sum + value * value
        pf = None
        for i in range(27):
            product = p[i] * fval[s, i, rows, :]
            pf = product if pf is None else pf + product
        terms[s, rows, :] = jnp.where(fluid, 3.0 * omega * omega * (pf - rho * total), 0.0)
        acc_ref[s] += square_sum

    acc_ref[...] = jnp.zeros_like(acc_ref)
    pack(0)
    pl.semaphore_wait(barrier, len(greeted))

    sent = []
    for s in range(steps):
        moving = copies(s)
        sent += moving
        for copy in moving[:2]:
            copy.start()
        if s > 0:
            pack(s)
        for copy in moving[2:]:
            copy.start()
        if s == 0:
            for copy in loads[1:]:
                copy.wait()
        base_moments(s)
        for copy in moving[2:4]:
            copy.wait_recv()
        lax.fori_loop(1, nx - 1, lambda x, _, s=s: (step_plane(s, x), 0)[1], 0)
        for copy in moving[:2] + moving[4:]:
            copy.wait_recv()
        lax.fori_loop(0, 2, lambda t, _, s=s: (step_plane(s, t * (nx - 1)), 0)[1], 0)

    for x in range(nx):
        for i in range(27):
            adj_ref[i, x] = fld[steps, pl.ds((x + 1) * plane + i * ny, ny), :]
    outs = [
        pltpu.make_async_copy(adj_ref, raw_hbm, local_sem.at[0]),
        pltpu.make_async_copy(terms, terms_hbm, local_sem.at[1]),
    ]

    lane = lax.broadcasted_iota(jnp.int32, (1, nz), 1)
    row = jnp.zeros((1, nz), jnp.float32)
    for s in range(steps):
        value = jnp.sum(jnp.sum(acc_ref[s], axis=0, keepdims=True), axis=1, keepdims=True)
        row = row + jnp.where(lane == s, value, 0.0)
    own[0] = row
    moving = [
        pltpu.make_async_remote_copy(
            src_ref=own.at[0],
            dst_ref=line.at[here],
            send_sem=sum_send.at[k],
            recv_sem=sum_recv.at[k],
            device_id=device,
            device_id_type=MESH,
        )
        for k, device in enumerate(others)
    ]
    for copy in moving:
        copy.start()
    sent += moving
    for copy in outs:
        copy.start()
    for copy in moving:
        copy.wait_recv()
    line[here] = row
    row = line[0]
    for k in range(1, every):
        row = row + line[k]
    own[1] = row
    last_copy = pltpu.make_async_copy(own.at[1], sums_hbm, local_sem.at[2])
    last_copy.start()
    for copy in sent:
        copy.wait_send()
    for copy in outs:
        copy.wait()
    last_copy.wait()


def finish(
    steps, entries, parts,
    raw_hbm, terms_hbm, sums_hbm, out_hbm, sens_hbm, growth_ref,
    raw, terms, sums, sens, load_sem, store_sem,
):
    cut = raw.shape[0] // parts
    small = [
        pltpu.make_async_copy(sums_hbm, sums, load_sem.at[parts]),
        pltpu.make_async_copy(terms_hbm, terms, load_sem.at[parts + 1]),
    ]
    pieces = [pl.ds(k * cut, cut) for k in range(parts)]
    loads = [
        pltpu.make_async_copy(raw_hbm.at[piece], raw.at[piece], load_sem.at[k])
        for k, piece in enumerate(pieces)
    ]
    for copy in small + loads:
        copy.start()
    stores = [
        pltpu.make_async_copy(raw.at[piece], out_hbm.at[piece], store_sem.at[k])
        for k, piece in enumerate(pieces)
    ]
    stores.append(pltpu.make_async_copy(sens, sens_hbm, store_sem.at[parts]))
    for copy in small:
        copy.wait()
    row = sums[...]
    lane = lax.broadcasted_iota(jnp.int32, row.shape, 1)
    inverse = jnp.ones(row.shape, jnp.float32)
    total = jnp.zeros(sens.shape, jnp.float32)
    factors = []
    for s in range(steps):
        total = total + terms[s] * inverse
        value = jnp.sum(jnp.where(lane == s, row, 0.0), axis=1, keepdims=True)
        value = jnp.broadcast_to(value, row.shape)
        factors.append(jnp.sqrt(value * (inverse * inverse) * (1.0 / entries) + 1e-06))
        inverse = inverse / factors[-1]
    sens[...] = total
    stores[parts].start()
    for k, piece in enumerate(pieces):
        loads[k].wait()
        raw[piece] = raw[piece] * inverse.reshape((1, 1, 1, -1))
        stores[k].start()
    for s in range(steps):
        growth_ref[s] = factors[s][0, 0]
    for copy in stores:
        copy.wait()


def body(checkpoints, step_ckpt, solid_mask, omega, adjoint_init):
    nck, _, nx, ny, nz = checkpoints.shape
    steps = step_ckpt.shape[0]
    ngx, ngy = lax.axis_size("gx"), lax.axis_size("gy")
    f32 = jnp.float32
    hbm = pl.BlockSpec(memory_space=pltpu.HBM)
    dma = pltpu.SemaphoreType.DMA
    rows = (nx + 2) * 27 * ny
    others = ngx * ngy - 1
    raw, terms, sums = pl.pallas_call(
        functools.partial(kernel, steps, nx, ny, nz, ngx, ngy),
        out_shape=(
            jax.ShapeDtypeStruct(adjoint_init.shape, f32),
            jax.ShapeDtypeStruct((steps, nx * ny, nz), f32),
            jax.ShapeDtypeStruct((1, nz), f32),
        ),
        in_specs=[hbm, hbm, hbm, hbm, hbm],
        out_specs=(hbm, hbm, hbm),
        scratch_shapes=[
            pltpu.SMEM((steps,), jnp.int32),
            pltpu.VMEM((nck, 27, nx * ny, nz), checkpoints.dtype),
            pltpu.VMEM((nx * ny, nz), jnp.int32),
            pltpu.VMEM((nx * ny, nz), f32),
            pltpu.VMEM(adjoint_init.shape, f32),
            pltpu.VMEM((steps + 1, rows, nz), f32),
            pltpu.VMEM((steps, 2, nx * EDGE, nz), f32),
            pltpu.VMEM((steps, 2, (nx + 2) * EDGE, nz), f32),
            pltpu.VMEM((steps, 27, nx * ny, nz), f32),
            pltpu.VMEM((steps, 4, nx * ny, nz), f32),
            pltpu.VMEM((steps, nx * ny, nz), f32),
            pltpu.VMEM((steps, ny, nz), f32),
            pltpu.VMEM((others + 1, 1, nz), f32),
            pltpu.VMEM((2, 1, nz), f32),
            dma((5,)),
            dma((steps, 8)),
            dma((steps, 8)),
            dma((others,)),
            dma((others,)),
        ],
        compiler_params=pltpu.CompilerParams(
            collective_id=0, has_side_effects=True, vmem_limit_bytes=60 * 1024 * 1024
        ),
        cost_estimate=pl.CostEstimate(flops=10**7, bytes_accessed=2 * 10**6, transcendentals=0),
    )(
        step_ckpt,
        checkpoints.reshape(nck, 27, nx * ny, nz),
        solid_mask.reshape(nx * ny, nz),
        omega.reshape(nx * ny, nz),
        adjoint_init,
    )
    parts = 3
    out, sens, growth = pl.pallas_call(
        functools.partial(finish, steps, float(adjoint_init.size * ngx * ngy), parts),
        out_shape=(
            jax.ShapeDtypeStruct(adjoint_init.shape, f32),
            jax.ShapeDtypeStruct((nx * ny, nz), f32),
            jax.ShapeDtypeStruct((steps,), f32),
        ),
        in_specs=[hbm, hbm, hbm],
        out_specs=(hbm, hbm, pl.BlockSpec(memory_space=pltpu.SMEM)),
        scratch_shapes=[
            pltpu.VMEM(adjoint_init.shape, f32),
            pltpu.VMEM((steps, nx * ny, nz), f32),
            pltpu.VMEM((1, nz), f32),
            pltpu.VMEM((nx * ny, nz), f32),
            dma((parts + 2,)),
            dma((parts + 1,)),
        ],
        compiler_params=pltpu.CompilerParams(vmem_limit_bytes=60 * 1024 * 1024),
        cost_estimate=pl.CostEstimate(flops=10**5, bytes_accessed=10**6, transcendentals=0),
    )(raw, terms, sums)
    return out, sens.reshape(omega.shape), growth


def solution(mesh):
    in_specs = (
        P(None, None, "gx", "gy", None),
        P(),
        P("gx", "gy", None),
        P("gx", "gy", None),
        P(None, "gx", "gy", None),
    )
    out_specs = (P(None, "gx", "gy", None), P("gx", "gy", None), P())
    return jax.shard_map(body, mesh=mesh, in_specs=in_specs, out_specs=out_specs, check_vma=False)
```

```python
import functools

import jax
import jax.numpy as jnp
from jax import lax
from jax.experimental import pallas as pl
from jax.experimental.pallas import tpu as pltpu
from jax.sharding import PartitionSpec as P

MESH = pl.DeviceIdType.MESH
EDGE = 16
CORNERS = ((0, 0), (0, 1), (1, 0), (1, 1))


def three(minus, plain, plus):
    even = plus + minus
    return 4.0 * plain + even, plus - minus, even


def weighted_moments(p):
    along_z = [three(*p[3 * k : 3 * k + 3]) for k in range(9)]
    along_y = []
    for a in range(3):
        rows = along_z[3 * a : 3 * a + 3]
        y0 = three(*[r[0] for r in rows])
        y1 = three(*[r[1] for r in rows])
        y2 = three(*[r[2] for r in rows])
        along_y.append((y0[0], y0[1], y0[2], y1[0], y1[1], y2[0]))
    m, my, myy, mz, myz, mzz = (three(*[r[k] for r in along_y]) for k in range(6))
    return m[0], m[1], my[0], mz[0], m[2], myy[0], mzz[0], my[1], mz[1], myz[0]


def plain_moments(f):
    zs = [(f[3 * k] + f[3 * k + 2] + f[3 * k + 1], f[3 * k + 2] - f[3 * k]) for k in range(9)]
    ys = []
    for a in range(3):
        r = zs[3 * a : 3 * a + 3]
        ys.append((r[0][0] + r[2][0] + r[1][0], r[2][0] - r[0][0], r[0][1] + r[1][1] + r[2][1]))
    total = [ys[0][k] + ys[1][k] + ys[2][k] for k in range(3)]
    return total[0], ys[2][0] - ys[0][0], total[1], total[2]


def kernel(
    steps, nx, ny, nz, ngx, ngy,
    idx_hbm, ck_hbm, solid_hbm, omega_hbm, adj_hbm,
    raw_hbm, terms_hbm, sums_hbm,
    idx_ref, ck_ref, solid_ref, omega_ref, adj_ref,
    fld, ysend, yrecv, fval, mom, terms, acc_ref, line, own,
    local_sem, send_sem, recv_sem, sum_send, sum_recv,
):
    gx, gy = lax.axis_index("gx"), lax.axis_index("gy")
    plane = 27 * ny

    def gxs(k):
        return lax.rem(gx + (k + ngx), ngx)

    def gys(k):
        return lax.rem(gy + (k + ngy), ngy)

    loads = [
        pltpu.make_async_copy(src, dst, local_sem.at[n])
        for n, (src, dst) in enumerate(
            (
                (adj_hbm, adj_ref),
                (ck_hbm, ck_ref),
                (solid_hbm, solid_ref),
                (omega_hbm, omega_ref),
                (idx_hbm, idx_ref),
            )
        )
    ]
    barrier = pltpu.get_barrier_semaphore()
    here = gx * ngy + gy
    every = ngx * ngy
    others = []
    for k in range(1, every):
        there = lax.rem(here + k, every)
        others.append((there // ngy, lax.rem(there, ngy)))
    greeted = others
    for device in greeted:
        pl.semaphore_signal(barrier, inc=1, device_id=device, device_id_type=MESH)

    for copy in loads:
        copy.start()
    loads[0].wait()
    for x in range(nx):
        for i in range(27):
            fld[0, pl.ds((x + 1) * plane + i * ny, ny), :] = adj_ref[i, x]

    def pack(s):
        for x in range(nx):
            for d in (0, 1):
                row = 0 if d == 1 else ny - 1
                for a in range(3):
                    start = (x + 1) * plane + (9 * a + 6 * d) * ny + row
                    ysend[s, d, pl.ds(x * EDGE + 4 * a, 3), :] = fld[s, pl.ds(start, 3, stride=ny), :]

    def copies(s):
        todo = [
            (fld.at[s, pl.ds(nx * plane, 9 * ny), :], fld.at[s, pl.ds(0, 9 * ny), :], (gxs(1), gy)),
            (
                fld.at[s, pl.ds(plane + 18 * ny, 9 * ny), :],
                fld.at[s, pl.ds((nx + 1) * plane + 18 * ny, 9 * ny), :],
                (gxs(-1), gy),
            ),
        ]
        for d in (0, 1):
            todo.append(
                (ysend.at[s, d], yrecv.at[s, d, pl.ds(EDGE, nx * EDGE), :], (gx, gys(1 - 2 * d)))
            )
        for a, d in CORNERS:
            src = 8 if a else (nx - 1) * EDGE
            dst = (nx + 1) * EDGE + 8 if a else 0
            todo.append(
                (
                    ysend.at[s, d, pl.ds(src, 8), :],
                    yrecv.at[s, d, pl.ds(dst, 8), :],
                    (gxs(1 - 2 * a), gys(1 - 2 * d)),
                )
            )
        return [
            pltpu.make_async_remote_copy(
                src_ref=src,
                dst_ref=dst,
                send_sem=send_sem.at[s, n],
                recv_sem=recv_sem.at[s, n],
                device_id=device,
                device_id_type=MESH,
            )
            for n, (src, dst, device) in enumerate(todo)
        ]

    def base_moments(s):
        which = idx_ref[s]

        def pair(k, _):
            rows = pl.ds(pl.multiple_of(k * 2 * ny, 2 * ny), 2 * ny)
            f = [ck_ref[which, i, rows, :].astype(jnp.float32) for i in range(27)]
            for i in range(27):
                fval[s, i, rows, :] = f[i]
            rho, jx, jy, jz = plain_moments(f)
            inv = 1.0 / rho
            for n, value in enumerate((rho, jx * inv, jy * inv, jz * inv)):
                mom[s, n, rows, :] = value
            return 0

        lax.fori_loop(0, nx // 2, pair, 0)

    lane_row = lax.broadcasted_iota(jnp.int32, (ny, nz), 0)
    first, last = lane_row == 0, lane_row == ny - 1

    def step_plane(s, x):
        p = []
        for i in range(27):
            a, b, c = i // 9, i // 3 % 3, i % 3
            start = pl.multiple_of((x + a) * plane + i * ny, ny)
            tile = fld[s, pl.ds(start, ny), :]
            if b != 1:
                edge = yrecv[s, b // 2, pl.ds((x + a) * EDGE + 4 * a + c, 1), :]
                tile = jnp.where(first if b == 2 else last, jnp.broadcast_to(edge, (ny, nz)), tile)
                tile = pltpu.roll(tile, ny - 1 if b == 2 else 1, 0)
            if c != 1:
                tile = pltpu.roll(tile, nz - 1 if c == 2 else 1, 1)
            p.append(tile)
        rows = pl.ds(pl.multiple_of(x * ny, ny), ny)
        rho, ux, uy, uz = (mom[s, n, rows, :] for n in range(4))
        omega = omega_ref[rows, :]
        fluid = solid_ref[rows, :] == 0
        m0, mx, my, mz, mxx, myy, mzz, mxy, mxz, myz = weighted_moments(p)
        vx = mxx * ux + mxy * uy + mxz * uz
        vy = mxy * ux + myy * uy + myz * uz
        vz = mxz * ux + myz * uy + mzz * uz
        square = ux * ux + uy * uy + uz * uz
        um = ux * mx + uy * my + uz * mz
        uv = ux * vx + uy * vy + uz * vz
        scale = 1.0 / 216.0
        total = scale * (m0 * (1.0 - 1.5 * square) + 3.0 * um + 4.5 * uv)
        gxv = scale * (3.0 * (mx - ux * m0) + 9.0 * vx)
        gyv = scale * (3.0 * (my - uy * m0) + 9.0 * vy)
        gzv = scale * (3.0 * (mz - uz * m0) + 9.0 * vz)
        base = omega * (total - (ux * gxv + uy * gyv + uz * gzv))
        wx, wy, wz = omega * gxv, omega * gyv, omega * gzv
        keep = 1.0 - omega
        square_sum = None
        for a in range(3):
            ta = base if a == 1 else (base + wx if a == 2 else base - wx)
            for b in range(3):
                tb = ta if b == 1 else (ta + wy if b == 2 else ta - wy)
                for c in range(3):
                    tc = tb if c == 1 else (tb + wz if c == 2 else tb - wz)
                    i = 9 * a + 3 * b + c
                    value = jnp.where(fluid, keep * p[i] + tc, p[26 - i])
                    start = pl.multiple_of((x + 1) * plane + i * ny, ny)
                    fld[s + 1, pl.ds(start, ny), :] = value
                    square_sum = value * value if square_sum is None else square_sum + value * value
        pf = None
        for i in range(27):
            product = p[i] * fval[s, i, rows, :]
            pf = product if pf is None else pf + product
        terms[s, rows, :] = jnp.where(fluid, 3.0 * omega * omega * (pf - rho * total), 0.0)
        acc_ref[s] += square_sum

    acc_ref[...] = jnp.zeros_like(acc_ref)
    pack(0)
    pl.semaphore_wait(barrier, len(greeted))

    sent = []
    for s in range(steps):
        moving = copies(s)
        sent += moving
        for copy in moving[:2]:
            copy.start()
        if s > 0:
            pack(s)
        for copy in moving[2:]:
            copy.start()
        if s == 0:
            for copy in loads[1:]:
                copy.wait()
        base_moments(s)
        for copy in moving[2:4]:
            copy.wait_recv()
        lax.fori_loop(1, nx - 1, lambda x, _, s=s: (step_plane(s, x), 0)[1], 0)
        for copy in moving[:2] + moving[4:]:
            copy.wait_recv()
        lax.fori_loop(0, 2, lambda t, _, s=s: (step_plane(s, t * (nx - 1)), 0)[1], 0)

    for x in range(nx):
        for i in range(27):
            adj_ref[i, x] = fld[steps, pl.ds((x + 1) * plane + i * ny, ny), :]
    outs = [
        pltpu.make_async_copy(adj_ref, raw_hbm, local_sem.at[0]),
        pltpu.make_async_copy(terms, terms_hbm, local_sem.at[1]),
    ]

    lane = lax.broadcasted_iota(jnp.int32, (1, nz), 1)
    row = jnp.zeros((1, nz), jnp.float32)
    for s in range(steps):
        value = jnp.sum(jnp.sum(acc_ref[s], axis=0, keepdims=True), axis=1, keepdims=True)
        row = row + jnp.where(lane == s, value, 0.0)
    own[0] = row
    moving = [
        pltpu.make_async_remote_copy(
            src_ref=own.at[0],
            dst_ref=line.at[here],
            send_sem=sum_send,
            recv_sem=sum_recv,
            device_id=device,
            device_id_type=MESH,
        )
        for device in others
    ]
    for copy in moving:
        copy.start()
    for copy in outs:
        copy.start()
    bulk = line.at[pl.ds(0, every - 1)]
    pltpu.make_async_copy(bulk, bulk, sum_recv).wait()
    line[here] = row
    row = line[0]
    for k in range(1, every):
        row = row + line[k]
    own[1] = row
    last_copy = pltpu.make_async_copy(own.at[1], sums_hbm, local_sem.at[2])
    last_copy.start()
    for copy in sent:
        copy.wait_send()
    pltpu.make_async_copy(bulk, bulk, sum_send).wait()
    for copy in outs:
        copy.wait()
    last_copy.wait()


def finish(
    steps, entries, parts,
    raw_hbm, terms_hbm, sums_hbm, out_hbm, sens_hbm, growth_ref,
    raw, terms, sums, sens, load_sem, store_sem,
):
    cut = raw.shape[0] // parts
    small = [
        pltpu.make_async_copy(sums_hbm, sums, load_sem.at[parts]),
        pltpu.make_async_copy(terms_hbm, terms, load_sem.at[parts + 1]),
    ]
    pieces = [pl.ds(k * cut, cut) for k in range(parts)]
    loads = [
        pltpu.make_async_copy(raw_hbm.at[piece], raw.at[piece], load_sem.at[k])
        for k, piece in enumerate(pieces)
    ]
    for copy in small + loads:
        copy.start()
    stores = [
        pltpu.make_async_copy(raw.at[piece], out_hbm.at[piece], store_sem.at[k])
        for k, piece in enumerate(pieces)
    ]
    stores.append(pltpu.make_async_copy(sens, sens_hbm, store_sem.at[parts]))
    for copy in small:
        copy.wait()
    row = sums[...]
    lane = lax.broadcasted_iota(jnp.int32, row.shape, 1)
    inverse = jnp.ones(row.shape, jnp.float32)
    total = jnp.zeros(sens.shape, jnp.float32)
    factors = []
    for s in range(steps):
        total = total + terms[s] * inverse
        value = jnp.sum(jnp.where(lane == s, row, 0.0), axis=1, keepdims=True)
        value = jnp.broadcast_to(value, row.shape)
        factors.append(jnp.sqrt(value * (inverse * inverse) * (1.0 / entries) + 1e-06))
        inverse = inverse / factors[-1]
    sens[...] = total
    stores[parts].start()
    for k, piece in enumerate(pieces):
        loads[k].wait()
        raw[piece] = raw[piece] * inverse.reshape((1, 1, 1, -1))
        stores[k].start()
    for s in range(steps):
        growth_ref[s] = factors[s][0, 0]
    for copy in stores:
        copy.wait()


def body(checkpoints, step_ckpt, solid_mask, omega, adjoint_init):
    nck, _, nx, ny, nz = checkpoints.shape
    steps = step_ckpt.shape[0]
    ngx, ngy = lax.axis_size("gx"), lax.axis_size("gy")
    f32 = jnp.float32
    hbm = pl.BlockSpec(memory_space=pltpu.HBM)
    dma = pltpu.SemaphoreType.DMA
    rows = (nx + 2) * 27 * ny
    others = ngx * ngy - 1
    raw, terms, sums = pl.pallas_call(
        functools.partial(kernel, steps, nx, ny, nz, ngx, ngy),
        out_shape=(
            jax.ShapeDtypeStruct(adjoint_init.shape, f32),
            jax.ShapeDtypeStruct((steps, nx * ny, nz), f32),
            jax.ShapeDtypeStruct((1, nz), f32),
        ),
        in_specs=[hbm, hbm, hbm, hbm, hbm],
        out_specs=(hbm, hbm, hbm),
        scratch_shapes=[
            pltpu.SMEM((steps,), jnp.int32),
            pltpu.VMEM((nck, 27, nx * ny, nz), checkpoints.dtype),
            pltpu.VMEM((nx * ny, nz), jnp.int32),
            pltpu.VMEM((nx * ny, nz), f32),
            pltpu.VMEM(adjoint_init.shape, f32),
            pltpu.VMEM((steps + 1, rows, nz), f32),
            pltpu.VMEM((steps, 2, nx * EDGE, nz), f32),
            pltpu.VMEM((steps, 2, (nx + 2) * EDGE, nz), f32),
            pltpu.VMEM((steps, 27, nx * ny, nz), f32),
            pltpu.VMEM((steps, 4, nx * ny, nz), f32),
            pltpu.VMEM((steps, nx * ny, nz), f32),
            pltpu.VMEM((steps, ny, nz), f32),
            pltpu.VMEM((others + 1, 1, nz), f32),
            pltpu.VMEM((2, 1, nz), f32),
            dma((5,)),
            dma((steps, 8)),
            dma((steps, 8)),
            dma,
            dma,
        ],
        compiler_params=pltpu.CompilerParams(
            collective_id=0, has_side_effects=True, vmem_limit_bytes=60 * 1024 * 1024
        ),
        cost_estimate=pl.CostEstimate(flops=10**7, bytes_accessed=2 * 10**6, transcendentals=0),
    )(
        step_ckpt,
        checkpoints.reshape(nck, 27, nx * ny, nz),
        solid_mask.reshape(nx * ny, nz),
        omega.reshape(nx * ny, nz),
        adjoint_init,
    )
    parts = 3
    out, sens, growth = pl.pallas_call(
        functools.partial(finish, steps, float(adjoint_init.size * ngx * ngy), parts),
        out_shape=(
            jax.ShapeDtypeStruct(adjoint_init.shape, f32),
            jax.ShapeDtypeStruct((nx * ny, nz), f32),
            jax.ShapeDtypeStruct((steps,), f32),
        ),
        in_specs=[hbm, hbm, hbm],
        out_specs=(hbm, hbm, pl.BlockSpec(memory_space=pltpu.SMEM)),
        scratch_shapes=[
            pltpu.VMEM(adjoint_init.shape, f32),
            pltpu.VMEM((steps, nx * ny, nz), f32),
            pltpu.VMEM((1, nz), f32),
            pltpu.VMEM((nx * ny, nz), f32),
            dma((parts + 2,)),
            dma((parts + 1,)),
        ],
        compiler_params=pltpu.CompilerParams(vmem_limit_bytes=60 * 1024 * 1024),
        cost_estimate=pl.CostEstimate(flops=10**5, bytes_accessed=10**6, transcendentals=0),
    )(raw, terms, sums)
    return out, sens.reshape(omega.shape), growth


def solution(mesh):
    in_specs = (
        P(None, None, "gx", "gy", None),
        P(),
        P("gx", "gy", None),
        P("gx", "gy", None),
        P(None, "gx", "gy", None),
    )
    out_specs = (P(None, "gx", "gy", None), P("gx", "gy", None), P())
    return jax.shard_map(body, mesh=mesh, in_specs=in_specs, out_specs=out_specs, check_vma=False)
```
